32 devices in a mesh: pool: 2 (over core), seq: 4 (over y, x), dp: 4 (over z).
Axes of the slice: x: 2, y: 2, z: 4, core: 2. Of those that a mesh axis runs over, the one named last changes fastest.
Arguments:
- starting_latents: bfloat16 [8, 64, 512], P(('pool', 'dp'), None, 'seq'), may hold values from -6 to 6
- noise: bfloat16 [8, 8, 64, 512], P(('pool', 'dp'), None, None, 'seq'), may hold values from -6 to 6
- velocity_matrix: float32 [64, 64], replicated, may hold values from -0.75 to 0.75
- kept_rollout_steps: int32 [8, 2], replicated, may hold values from 1 to 8, as said below
- trainer_group_of: int32 [2, 4], replicated, may hold values from 0 to 3, each once within a row
- video_valid_tokens: int32 [8], replicated, may hold values from 128 to 512, as said below
- block_input_states: bfloat16 [8, 512, 3072], P(('pool', 'dp'), 'seq'), may hold values from -6 to 6
- upstream: bfloat16 [8, 2, 512, 2048], P(('pool', 'dp'), None, 'seq'), may hold values from -0.0625 to 0.0625
- patch_embed_weight: bfloat16 [64, 3072], replicated, may hold values from -0.75 to 0.75
- modulation: float32 [2, 8, 3072], replicated, may hold values from -1.5 to 1.5
- frozen_query_key_value: bfloat16 [3072, 6144], P(('pool', 'dp')), may hold values from -0.109375 to 0.109375
- query_down_factor: bfloat16 [3072, 128], replicated, may hold values from -0.109375 to 0.109375
- query_up_factor: bfloat16 [128, 2048], replicated, may hold values from -0.5 to 0.5
Outputs:
- grad_down: float32 [3072, 128], P('dp')
- grad_up: float32 [128, 2048], P(None, 'dp')
- final_latent: float32 [8, 64, 512], P(('pool', 'dp'), None, 'seq')
The draws below stay inside these ranges and needn't reach their ends.
Inputs may be any that keep to these rules, and one draw needn't show every extreme that they name: `kept_rollout_steps`: the 2 entries of a row are distinct. `trainer_group_of`: each row names every group once. `video_valid_tokens`: tokens of a video at positions from this count on are padding; some video is full.
All inputs are finite; a program needn't handle non-finite values.
Results may differ from the reference program's by a relative error of at most 0.0088.
Values may be sent and summed in bfloat16 or wider, within the bound.
A program may use at most 128 MiB of HBM per device.

```python
import math
import jax
import jax.numpy as jnp
from jax import lax

MODEL_WIDTH = 3072
HEADS = 16
HEAD_DIM = 128
UPDATE_RANK = 128
CHANNELS = 64
STEPS = 8
KEEP = 2
SEQ = 512
HALVES = 2
GROUPS = 4
VIDEOS = 8
ATTENTION_WIDTH = 2048


def draw_kept_rollout_steps(key, part):
    key = jax.random.fold_in(key, 11)
    scores = jax.random.randint(key, (VIDEOS, STEPS), 0, 1 << 20) * STEPS + jnp.arange(STEPS, dtype=jnp.int32)[None, :]
    order = jnp.argsort(scores, axis=1, stable=True)
    return (order[:, :KEEP] + 1).astype(jnp.int32)


def draw_video_valid_tokens(key, part):
    key = jax.random.fold_in(key, 23)
    first_key, second_key = jax.random.split(key)
    counts = jax.random.randint(first_key, (VIDEOS,), SEQ // 4, SEQ + 1)
    chosen = jax.random.randint(second_key, (), 0, VIDEOS)
    return jnp.where(jnp.arange(VIDEOS, dtype=jnp.int32) == chosen, SEQ, counts).astype(jnp.int32)


def levels(own_key, shape, shards, smallest, high):
    def one(dim, parts):
        steps = jax.random.uniform(jax.random.fold_in(jax.random.fold_in(own_key, 6), dim), (parts,), jnp.float32, smallest / len(shards), high / len(shards))
        return jnp.repeat(jnp.exp(steps), shape[dim] // parts).reshape((-1,) + (1,) * (len(shape) - dim - 1))

    loudness = one(*shards[0])
    for cut in shards[1:]:
        loudness = loudness * one(*cut)
    return loudness


def scatter_about(own_key, dims, scale, reach, shards=(), kind=jnp.bfloat16):
    values = jax.random.normal(own_key, dims, jnp.float32) * scale
    if len(shards) > 0:
        values = levels(own_key, dims, shards, -0.22, 0.18) * values
    return jnp.clip(values, min=-reach, max=reach).astype(kind)


def setup_inputs(seed: int = 0) -> dict:
    arg_keys = jax.random.split(jax.random.key(seed), 14)
    starting_latents = scatter_about(arg_keys[0], (VIDEOS, CHANNELS, SEQ), 1.0, 6.0, ((0, 8), (2, 4)))
    noise = scatter_about(arg_keys[1], (VIDEOS, STEPS, CHANNELS, SEQ), 1.0, 6.0, ((0, 8), (3, 4)))
    velocity_matrix = scatter_about(arg_keys[2], (CHANNELS, CHANNELS), CHANNELS ** -0.5, 0.75, (), jnp.float32)
    kept_rollout_steps = draw_kept_rollout_steps(jax.random.fold_in(arg_keys[13], 71), 0)
    trainer_group_of = jax.vmap(lambda own: jax.random.permutation(own, GROUPS))(jax.random.split(arg_keys[4], HALVES)).reshape((HALVES, GROUPS)).astype(jnp.int32)
    video_valid_tokens = draw_video_valid_tokens(jax.random.fold_in(arg_keys[13], 71), 0)
    block_input_states = scatter_about(arg_keys[6], (VIDEOS, SEQ, MODEL_WIDTH), 1.0, 6.0, ((0, 8), (1, 4)))
    upstream = scatter_about(arg_keys[7], (VIDEOS, KEEP, SEQ, ATTENTION_WIDTH), ((VIDEOS * KEEP * SEQ) ** -0.5), 0.0625, ((0, 8), (2, 4)))
    patch_embed_weight = scatter_about(arg_keys[8], (CHANNELS, MODEL_WIDTH), CHANNELS ** -0.5, 0.75)
    modulation = scatter_about(arg_keys[9], (2, STEPS, MODEL_WIDTH), 0.3, 1.5, (), jnp.float32)
    frozen_query_key_value = scatter_about(arg_keys[10], (MODEL_WIDTH, 3 * ATTENTION_WIDTH), MODEL_WIDTH ** -0.5, 0.109375, ((0, 8),))
    query_down_factor = scatter_about(arg_keys[11], (MODEL_WIDTH, UPDATE_RANK), MODEL_WIDTH ** -0.5, 0.109375)
    query_up_factor = scatter_about(arg_keys[12], (UPDATE_RANK, ATTENTION_WIDTH), UPDATE_RANK ** -0.5, 0.5)
    return dict(starting_latents=starting_latents, noise=noise, velocity_matrix=velocity_matrix, kept_rollout_steps=kept_rollout_steps, trainer_group_of=trainer_group_of, video_valid_tokens=video_valid_tokens, block_input_states=block_input_states, upstream=upstream, patch_embed_weight=patch_embed_weight, modulation=modulation, frozen_query_key_value=frozen_query_key_value, query_down_factor=query_down_factor, query_up_factor=query_up_factor)


epsilon = 1e-06
noise_level = 0.5

def norm_rows(values):
    return values * lax.rsqrt(lax.optimization_barrier(jnp.mean(values * values, -1, keepdims=True)) + epsilon)

def layer_norm(values):
    centered = values - lax.optimization_barrier(jnp.mean(values, -1, keepdims=True))
    return centered * lax.rsqrt(lax.optimization_barrier(jnp.mean(centered * centered, -1, keepdims=True)) + epsilon)

def norm_backward(raw, grad_normed):
    inverse = lax.rsqrt(lax.optimization_barrier(jnp.mean(raw * raw, -1, keepdims=True)) + epsilon)
    normal = raw * inverse
    gradient = grad_normed.astype(jnp.float32)
    inner_mean = lax.optimization_barrier(jnp.mean(gradient * normal, -1, keepdims=True))
    return (inverse * (gradient - normal * inner_mean)).astype(jnp.bfloat16)

def attend_head(query, keys, values, gradient_output, token_length):
    total_rows = query.shape[0]
    block_rows = 512 if total_rows % 512 == 0 else total_rows
    positions = jnp.arange(total_rows, dtype=jnp.int32)
    key_mask = (positions < token_length).astype(jnp.float32)
    factor = query.shape[1] ** (-0.5)

    def one_block(number):
        begin = (number * block_rows).astype(jnp.int32)
        query_rows = lax.dynamic_slice_in_dim(query, begin, block_rows, 0)
        grad_rows = lax.dynamic_slice_in_dim(gradient_output, begin, block_rows, 0)
        row_mask = (begin + jnp.arange(block_rows, dtype=jnp.int32) < token_length).astype(grad_rows.dtype)
        grad_rows = grad_rows * row_mask[:, None]
        scores = lax.dot_general(query_rows, keys, (((1,), (1,)), ((), ())), preferred_element_type=jnp.float32) * factor
        weights = jnp.exp(scores) * key_mask[None, :]
        probs = weights / lax.optimization_barrier(jnp.sum(weights, -1, keepdims=True))
        output = jnp.dot(probs.astype(jnp.bfloat16), values, preferred_element_type=jnp.float32)
        row_delta = lax.optimization_barrier(jnp.sum(grad_rows.astype(jnp.float32) * output, -1, keepdims=True))
        grad_probs = lax.dot_general(grad_rows, values, (((1,), (1,)), ((), ())), preferred_element_type=jnp.float32)
        grad_scores = (probs * (grad_probs - row_delta)).astype(jnp.bfloat16)
        return (jnp.dot(grad_scores, keys, preferred_element_type=jnp.float32) * factor).astype(jnp.bfloat16)
    blocks = lax.map(one_block, jnp.arange(total_rows // block_rows, dtype=jnp.int32))
    return blocks.reshape(total_rows, query.shape[1])

def attend_all(query, keys, values, gradient_output, token_length):
    samples, total_rows, head_count, head_width = query.shape

    def flatten(array):
        return jnp.transpose(array, (0, 2, 1, 3)).reshape(samples * head_count, total_rows, head_width)

    def per_head(group):
        return attend_head(group[0], group[1], group[2], group[3], token_length)
    result = lax.map(per_head, (flatten(query), flatten(keys), flatten(values), flatten(gradient_output)))
    return jnp.transpose(result.reshape(samples, head_count, total_rows, head_width), (0, 2, 1, 3))

def training_slot(kept_rows, rollout_steps, token_length, hidden_input, gradient_output, patch_embed_weight, modulation, frozen_query_key_value, query_down_factor, query_up_factor):
    embedded = jnp.einsum('kcs,cd->ksd', kept_rows.astype(jnp.float32), patch_embed_weight.astype(jnp.float32))
    hidden = hidden_input.astype(jnp.float32)[None] + embedded
    rows_index = (rollout_steps - 1).astype(jnp.int32)
    mod_scale = modulation[0][rows_index]
    mod_shift = modulation[1][rows_index]
    normed = (layer_norm(hidden) * (1.0 + mod_scale[:, None, :]) + mod_shift[:, None, :]).astype(jnp.bfloat16)
    flattened_rows = normed.reshape(KEEP * SEQ, MODEL_WIDTH)
    projected_rows = jnp.dot(flattened_rows, frozen_query_key_value, preferred_element_type=jnp.float32)
    lowrank_product = jnp.dot(flattened_rows, query_down_factor, preferred_element_type=jnp.float32).astype(jnp.bfloat16)
    query_unscaled = projected_rows[:, :ATTENTION_WIDTH] + jnp.dot(lowrank_product, query_up_factor, preferred_element_type=jnp.float32)
    query_unscaled = query_unscaled.reshape(KEEP, SEQ, HEADS, HEAD_DIM)
    key_raw = projected_rows[:, ATTENTION_WIDTH:2 * ATTENTION_WIDTH].reshape(KEEP, SEQ, HEADS, HEAD_DIM)
    value_heads = projected_rows[:, 2 * ATTENTION_WIDTH:].astype(jnp.bfloat16).reshape(KEEP, SEQ, HEADS, HEAD_DIM)
    query_heads = norm_rows(query_unscaled).astype(jnp.bfloat16)
    key_heads = norm_rows(key_raw).astype(jnp.bfloat16)
    grad_heads = gradient_output.reshape(KEEP, SEQ, HEADS, HEAD_DIM)
    grad_normed = attend_all(query_heads, key_heads, value_heads, grad_heads, token_length)
    gradient_query = norm_backward(query_unscaled, grad_normed).reshape(KEEP * SEQ, ATTENTION_WIDTH)
    grad_up = jnp.dot(lowrank_product.T, gradient_query, preferred_element_type=jnp.float32)
    gradient_lowrank = jnp.dot(gradient_query, query_up_factor.T, preferred_element_type=jnp.float32)
    grad_down = jnp.dot(flattened_rows.astype(jnp.float32).T, gradient_lowrank, precision=lax.Precision.HIGHEST)
    return (grad_down, grad_up)

def reference(starting_latents, noise, velocity_matrix, kept_rollout_steps, trainer_group_of, video_valid_tokens, block_input_states, upstream, patch_embed_weight, modulation, frozen_query_key_value, query_down_factor, query_up_factor):
    step_size = 1.0 / STEPS
    trajectories = []
    finals = []
    for video in range(VIDEOS):
        state = starting_latents[video].astype(jnp.float32)
        states = [state]
        for step in range(STEPS):
            drift = jnp.dot(velocity_matrix, state, precision=lax.Precision.HIGHEST)
            state = state - step_size * drift + noise_level * math.sqrt(step_size) * noise[video, step].astype(jnp.float32)
            states.append(state)
        trajectories.append(jnp.stack(states))
        finals.append(state)
    final_latent = jnp.stack(finals)
    everything = jnp.stack(trajectories)
    grad_down = jnp.zeros((MODEL_WIDTH, UPDATE_RANK), jnp.float32)
    grad_up = jnp.zeros((UPDATE_RANK, ATTENTION_WIDTH), jnp.float32)
    for slot_index in range(VIDEOS):
        half = slot_index // GROUPS
        group = slot_index % GROUPS
        source_half = 1 - half
        source_group = jnp.argmax(trainer_group_of[source_half] == group).astype(jnp.int32)
        video = (source_half * GROUPS + source_group).astype(jnp.int32)
        rollout_steps = kept_rollout_steps[video]
        token_length = video_valid_tokens[video]
        kept_rows = everything[video][rollout_steps].astype(jnp.bfloat16)
        down_portion, up_portion = training_slot(kept_rows, rollout_steps, token_length, block_input_states[slot_index], upstream[slot_index], patch_embed_weight, modulation, frozen_query_key_value, query_down_factor, query_up_factor)
        grad_down = grad_down + down_portion
        grad_up = grad_up + up_portion
    return (grad_down, grad_up, final_latent)
```

```python
import math

import jax
import jax.numpy as jnp
from jax import lax
from jax.experimental import pallas as pl
from jax.experimental.pallas import tpu as pltpu
from jax.sharding import PartitionSpec as P

HEADS = 16
HEAD_DIM = 128


epsilon = 1e-06
noise_level = 0.5


def partner(block, axis, apart):
    count = lax.axis_size(axis)
    route = []
    for low in range(count):
        high = low | 1 << apart
        if high != low and high < count:
            route += [(low, high), (high, low)]
    return lax.ppermute(block, axis, route)


def norm_rows(values):
    return values * lax.rsqrt(jnp.mean(values * values, -1, keepdims=True) + epsilon)


def layer_norm(values):
    centered = values - jnp.mean(values, -1, keepdims=True)
    return centered * lax.rsqrt(jnp.mean(centered * centered, -1, keepdims=True) + epsilon)


def embed_kernel(kept_ref, inputs_ref, embed_ref, scale_ref, shift_ref, factor_ref, normed_ref, low_ref):
    embedded = lax.dot_general(
        kept_ref[0], embed_ref[...], (((0,), (0,)), ((), ())), preferred_element_type=jnp.float32
    )
    hidden = inputs_ref[...].astype(jnp.float32) + embedded
    normed = (layer_norm(hidden) * (1.0 + scale_ref[0]) + shift_ref[0]).astype(jnp.bfloat16)
    normed_ref[...] = normed
    low_ref[...] = jnp.dot(
        normed, factor_ref[...], preferred_element_type=jnp.float32
    ).astype(jnp.bfloat16)


def embed(kept, inputs, embed_weight, scale, shift, down_factor):
    keep_count, channels, total_rows = kept.shape
    width, rank = down_factor.shape
    block = 128
    blocks = total_rows // block
    whole = lambda *shape: pl.BlockSpec(shape, lambda k, b: (0,) * len(shape))
    one_row = pl.BlockSpec((1, 1, width), lambda k, b: (k, 0, 0))
    out_rows = lambda size: pl.BlockSpec((block, size), lambda k, b: (k * blocks + b, 0))
    return pl.pallas_call(
        embed_kernel,
        grid=(keep_count, blocks),
        in_specs=[
            pl.BlockSpec((1, channels, block), lambda k, b: (k, 0, b)),
            pl.BlockSpec((block, width), lambda k, b: (b, 0)),
            whole(channels, width),
            one_row,
            one_row,
            whole(width, rank),
        ],
        out_specs=[out_rows(width), out_rows(rank)],
        out_shape=[
            jax.ShapeDtypeStruct((keep_count * total_rows, width), jnp.bfloat16),
            jax.ShapeDtypeStruct((keep_count * total_rows, rank), jnp.bfloat16),
        ],
        compiler_params=pltpu.CompilerParams(vmem_limit_bytes=32 * 1024 * 1024),
        cost_estimate=pl.CostEstimate(
            flops=2 * keep_count * total_rows * width * (rank + channels),
            bytes_accessed=keep_count * total_rows * width * 4,
            transcendentals=0,
        ),
    )(kept, inputs, embed_weight, scale[:, None, :], shift[:, None, :], down_factor)


def attend_kernel(length_ref, q_ref, k_ref, v_ref, g_ref, low_ref, up_ref, dlow_ref, gup_ref):
    sample, head = pl.program_id(0), pl.program_id(1)
    total_rows = q_ref.shape[0]
    block_rows = min(512, total_rows)
    length = length_ref[0]
    factor = HEAD_DIM ** (-0.5)
    along = (((1,), (1,)), ((), ()))
    key_raw = k_ref[...]
    keys = norm_rows(key_raw).astype(jnp.bfloat16)
    values = v_ref[...].astype(jnp.bfloat16)
    up = up_ref[...]
    key_mask = lax.broadcasted_iota(jnp.int32, (1, total_rows), 1) < length
    for begin in range(0, total_rows, block_rows):
        rows = pl.ds(begin, block_rows)
        low = low_ref[rows, :]
        query = q_ref[rows, :] + jnp.dot(low, up, preferred_element_type=jnp.float32)
        inverse = lax.rsqrt(jnp.mean(query * query, -1, keepdims=True) + epsilon)
        normal = query * inverse
        row_mask = begin + lax.broadcasted_iota(jnp.int32, (block_rows, 1), 0) < length
        grad = jnp.where(row_mask, g_ref[0, rows, :].astype(jnp.float32), 0.0)
        grad_bf = grad.astype(jnp.bfloat16)
        scores = lax.dot_general(
            normal.astype(jnp.bfloat16), keys, along, preferred_element_type=jnp.float32
        )
        weights = jnp.where(key_mask, jnp.exp2(scores * (factor * math.log2(math.e))), 0.0)
        share = 1.0 / jnp.sum(weights, -1, keepdims=True)
        output = jnp.dot(
            weights.astype(jnp.bfloat16), values, preferred_element_type=jnp.float32
        )
        delta = jnp.sum(grad * output, -1, keepdims=True) * share
        grad_probs = lax.dot_general(
            grad_bf, values, along, preferred_element_type=jnp.float32
        )
        grad_scores = (weights * (grad_probs - delta)).astype(jnp.bfloat16)
        gradient = jnp.dot(grad_scores, keys, preferred_element_type=jnp.float32) * (share * factor)
        inner_mean = jnp.mean(gradient * normal, -1, keepdims=True)
        dquery = (inverse * (gradient - normal * inner_mean)).astype(jnp.bfloat16)
        part = lax.dot_general(dquery, up, along, preferred_element_type=jnp.float32)
        up_part = lax.dot_general(
            dquery, low, (((0,), (0,)), ((), ())), preferred_element_type=jnp.float32
        )

        @pl.when(head == 0)
        def _():
            dlow_ref[rows, :] = part

        @pl.when(head != 0)
        def _():
            dlow_ref[rows, :] += part

        place = pl.ds(pl.multiple_of(head * HEAD_DIM, HEAD_DIM), HEAD_DIM)

        @pl.when(jnp.logical_and(sample == 0, begin == 0))
        def _():
            gup_ref[place, :] = up_part

        @pl.when(jnp.logical_or(sample != 0, begin != 0))
        def _():
            gup_ref[place, :] += up_part


def attend(length, projected, grads, low, up):
    keep_count, total_rows, columns = grads.shape
    heads = columns // HEAD_DIM
    rank = up.shape[0]

    def column_block(first):
        return pl.BlockSpec((total_rows, HEAD_DIM), lambda k, h: (k, first + h))

    return pl.pallas_call(
        attend_kernel,
        grid=(keep_count, heads),
        in_specs=[
            pl.BlockSpec(memory_space=pltpu.SMEM),
            column_block(0),
            column_block(heads),
            column_block(2 * heads),
            pl.BlockSpec((1, total_rows, HEAD_DIM), lambda k, h: (k, 0, h)),
            pl.BlockSpec((total_rows, rank), lambda k, h: (k, 0)),
            pl.BlockSpec((rank, HEAD_DIM), lambda k, h: (0, h)),
        ],
        out_specs=[
            pl.BlockSpec((total_rows, rank), lambda k, h: (k, 0)),
            pl.BlockSpec((columns, rank), lambda k, h: (0, 0)),
        ],
        out_shape=[
            jax.ShapeDtypeStruct((keep_count * total_rows, rank), jnp.float32),
            jax.ShapeDtypeStruct((columns, rank), jnp.float32),
        ],
        compiler_params=pltpu.CompilerParams(vmem_limit_bytes=48 * 1024 * 1024),
    )(length, projected, projected, projected, grads, low, up)


def reduce_kernel(
    sizes, src_ref, down_ref, up_ref, in1, out2, in2, in3, send1, recv1, send2, recv2, send3, recv3
):
    pools, seqs, dps, rows, up_rows = sizes
    plane = pools * seqs
    per = seqs // dps
    wire = in1.dtype
    p, s, d = lax.axis_index("pool"), lax.axis_index("seq"), lax.axis_index("dp")
    me = p * seqs + s
    beside = [lax.rem(me + o, plane) for o in range(1, plane)]
    beside_id = [(j // seqs, lax.rem(j, seqs), d) for j in beside]
    across = [lax.rem(d + o, dps) for o in range(1, dps)]
    across_id = [(p, s, j) for j in across]
    barrier = pltpu.get_barrier_semaphore()
    for target in beside_id + across_id:
        pl.semaphore_signal(barrier, inc=1, device_id=target, device_id_type=pl.DeviceIdType.MESH)
    pl.semaphore_wait(barrier, plane - 1 + dps - 1)

    def copy(src, dst, send, recv, target):
        return pltpu.make_async_remote_copy(
            src_ref=src,
            dst_ref=dst,
            send_sem=send,
            recv_sem=recv,
            device_id=target,
            device_id_type=pl.DeviceIdType.MESH,
        )

    sends = []
    for j, target in zip(beside, beside_id):
        one = copy(src_ref.at[j], in1.at[me], send1.at[j], recv1.at[me], target)
        one.start()
        sends.append(one)
    in1[me] = src_ref[me]
    for j, target in zip(beside, beside_id):
        copy(src_ref.at[j], in1.at[j], send1.at[j], recv1.at[j], target).wait_recv()
    split = dps * rows
    total = in1[0, :split, :].astype(jnp.float32)
    for t in range(1, plane):
        total = total + in1[t, :split, :].astype(jnp.float32)
    for block in range(dps):
        ups = None
        for t in range(plane):
            if t % seqs // per == block:
                term = in1[t, split:, :].astype(jnp.float32)
                ups = term if ups is None else ups + term
        out2[block, :rows, :] = total[block * rows : (block + 1) * rows].astype(wire)
        out2[block, rows:, :] = ups.astype(wire)
    for j, target in zip(across, across_id):
        one = copy(out2.at[j], in2.at[d], send2.at[j], recv2.at[d], target)
        one.start()
        sends.append(one)
    in2[d] = out2[d]
    for j, target in zip(across, across_id):
        copy(out2.at[j], in2.at[j], send2.at[j], recv2.at[j], target).wait_recv()
    owned = in2[0].astype(jnp.float32)
    for t in range(1, dps):
        owned = owned + in2[t].astype(jnp.float32)
    in3[me] = owned.astype(wire)
    for j, target in zip(beside, beside_id):
        one = copy(in3.at[me], in3.at[me], send3.at[j], recv3.at[me], target)
        one.start()
        sends.append(one)
    for j, target in zip(beside, beside_id):
        copy(in3.at[j], in3.at[j], send3.at[j], recv3.at[j], target).wait_recv()
    for t in range(plane):
        down_ref[t * rows : (t + 1) * rows, :] = in3[t, :rows, :].astype(jnp.float32)
        up_ref[t * up_rows : (t + 1) * up_rows, :] = in3[t, rows:, :].astype(jnp.float32)
    for one in sends:
        one.wait_send()


def reduce_gradients(grad_down, grad_up_rows):
    pools, seqs, dps = (lax.axis_size(axis) for axis in ("pool", "seq", "dp"))
    plane = pools * seqs
    per = seqs // dps
    rank = grad_down.shape[1]
    down_rows = grad_down.shape[0] // dps
    own_up = grad_up_rows.shape[0]
    total_up = own_up * per
    rows, up_rows = down_rows // plane, total_up // plane
    wire = jnp.bfloat16 if rows % 16 == 0 and up_rows % 16 == 0 else jnp.float32
    if per > 1:
        here = lax.rem(lax.axis_index("seq"), per)
        grad_up_rows = lax.dynamic_update_slice_in_dim(
            jnp.zeros((total_up, rank), jnp.float32), grad_up_rows, here * own_up, 0
        )
    pieces = jnp.concatenate(
        [
            jnp.transpose(grad_down.reshape(dps, plane, rows, rank), (1, 0, 2, 3)).reshape(
                plane, dps * rows, rank
            ),
            grad_up_rows.reshape(plane, up_rows, rank),
        ],
        1,
    ).astype(wire)
    vmem = pl.BlockSpec(memory_space=pltpu.VMEM)
    dma = pltpu.SemaphoreType.DMA
    return pl.pallas_call(
        lambda *refs: reduce_kernel((pools, seqs, dps, rows, up_rows), *refs),
        in_specs=[vmem],
        out_specs=[vmem, vmem],
        out_shape=[
            jax.ShapeDtypeStruct((down_rows, rank), jnp.float32),
            jax.ShapeDtypeStruct((total_up, rank), jnp.float32),
        ],
        scratch_shapes=[
            pltpu.VMEM((plane, dps * rows + up_rows, rank), wire),
            pltpu.VMEM((dps, rows + up_rows, rank), wire),
            pltpu.VMEM((dps, rows + up_rows, rank), wire),
            pltpu.VMEM((plane, rows + up_rows, rank), wire),
            dma((plane,)),
            dma((plane,)),
            dma((dps,)),
            dma((dps,)),
            dma((plane,)),
            dma((plane,)),
        ],
        compiler_params=pltpu.CompilerParams(
            collective_id=1, has_side_effects=True, vmem_limit_bytes=48 * 1024 * 1024
        ),
    )(pieces)


def body(
    starting_latents,
    noise,
    velocity_matrix,
    kept_rollout_steps,
    trainer_group_of,
    video_valid_tokens,
    block_input_states,
    upstream,
    patch_embed_weight,
    modulation,
    frozen_query_key_value,
    query_down_factor,
    query_up_factor,
):
    halves = lax.axis_size("pool")
    groups = lax.axis_size("dp")
    half = lax.axis_index("pool")
    group = lax.axis_index("dp")
    videos = halves * groups
    video = half * groups + group
    video_ids = jnp.arange(videos, dtype=jnp.int32)
    steps_total = noise.shape[1]
    step_size = 1.0 / steps_total
    own_steps = jnp.sum(jnp.where((video_ids == video)[:, None], kept_rollout_steps, 0), 0)
    state = starting_latents[0].astype(jnp.float32)
    kept_rows = jnp.zeros((own_steps.shape[0],) + state.shape, jnp.float32)
    for step in range(steps_total):
        drift = jnp.dot(velocity_matrix, state, precision=lax.Precision.HIGHEST)
        state = (
            state
            - step_size * drift
            + noise_level * math.sqrt(step_size) * noise[0, step].astype(jnp.float32)
        )
        kept_rows = jnp.where((own_steps == step + 1)[:, None, None], state[None], kept_rows)
    kept_rows = kept_rows.astype(jnp.bfloat16)
    source_half = 1 - half
    trainer_row = jnp.sum(
        jnp.where(
            (jnp.arange(halves, dtype=jnp.int32) == source_half)[:, None], trainer_group_of, 0
        ),
        0,
    )
    source_group = jnp.sum(jnp.where(trainer_row == group, jnp.arange(groups, dtype=jnp.int32), 0))
    source = source_half * groups + source_group
    seqs = lax.axis_size("seq")
    place = lax.axis_index("seq")
    inner_width = query_up_factor.shape[1]
    columns = inner_width // seqs
    inputs_all = lax.all_gather(block_input_states[0], "seq", axis=0, tiled=True)
    grads_all = lax.all_to_all(upstream[0], "seq", split_axis=2, concat_axis=1, tiled=True)
    weight_rows = frozen_query_key_value.shape[0]
    own_weights = lax.dynamic_slice_in_dim(
        frozen_query_key_value.reshape(weight_rows, 3, inner_width), place * columns, columns, 2
    ).reshape(weight_rows, 3 * columns)
    weights = lax.all_gather(own_weights, ("pool", "dp"), axis=0, tiled=True)
    swapped = partner(kept_rows, "pool", 0)
    spread = lax.all_gather(swapped, ("dp", "seq"), axis=0)
    spread = spread.reshape((groups, seqs) + swapped.shape)
    received = lax.dynamic_index_in_dim(spread, source_group, 0, keepdims=False)
    received = jnp.transpose(received, (1, 2, 0, 3)).reshape(
        swapped.shape[0], swapped.shape[1], seqs * swapped.shape[2]
    )
    train_steps = jnp.sum(jnp.where((video_ids == source)[:, None], kept_rollout_steps, 0), 0)
    token_length = jnp.sum(jnp.where(video_ids == source, video_valid_tokens, 0))
    one_hot = (
        train_steps[:, None] - 1 == jnp.arange(steps_total, dtype=jnp.int32)[None, :]
    ).astype(jnp.float32)
    mod_scale = jnp.dot(one_hot, modulation[0], precision=lax.Precision.HIGHEST)
    mod_shift = jnp.dot(one_hot, modulation[1], precision=lax.Precision.HIGHEST)
    flattened_rows, low = embed(
        received, inputs_all, patch_embed_weight, mod_scale, mod_shift, query_down_factor
    )
    projected = jnp.dot(flattened_rows, weights, preferred_element_type=jnp.float32)
    own_up = lax.dynamic_slice_in_dim(query_up_factor, place * columns, columns, 1)
    gradient_low, grad_up_rows = attend(
        token_length.reshape(1), projected, grads_all, low, own_up
    )
    grad_down = lax.dot_general(
        flattened_rows,
        gradient_low.astype(jnp.bfloat16),
        (((0,), (0,)), ((), ())),
        preferred_element_type=jnp.float32,
    )
    owned_down, owned_up = reduce_gradients(grad_down, grad_up_rows)
    return (owned_down, owned_up.T, state[None])


def solution(mesh):
    return jax.shard_map(
        body,
        mesh=mesh,
        in_specs=(
            P(("pool", "dp"), None, "seq"),
            P(("pool", "dp"), None, None, "seq"),
            P(),
            P(),
            P(),
            P(),
            P(("pool", "dp"), "seq", None),
            P(("pool", "dp"), None, "seq", None),
            P(),
            P(),
            P(("pool", "dp"), None),
            P(),
            P(),
        ),
        out_specs=(P("dp", None), P(None, "dp"), P(("pool", "dp"), None, "seq")),
        check_vma=False,
    )
```

```python
import math

import jax
import jax.numpy as jnp
from jax import lax
from jax.experimental import pallas as pl
from jax.experimental.pallas import tpu as pltpu
from jax.sharding import PartitionSpec as P

HEADS = 16
HEAD_DIM = 128


epsilon = 1e-06
noise_level = 0.5


def partner(block, axis, apart):
    count = lax.axis_size(axis)
    route = []
    for low in range(count):
        high = low | 1 << apart
        if high != low and high < count:
            route += [(low, high), (high, low)]
    return lax.ppermute(block, axis, route)


def norm_rows(values):
    return values * lax.rsqrt(jnp.mean(values * values, -1, keepdims=True) + epsilon)


def layer_norm(values):
    centered = values - jnp.mean(values, -1, keepdims=True)
    return centered * lax.rsqrt(jnp.mean(centered * centered, -1, keepdims=True) + epsilon)


def embed_kernel(kept_ref, inputs_ref, embed_ref, scale_ref, shift_ref, factor_ref, normed_ref, low_ref):
    embedded = lax.dot_general(
        kept_ref[0], embed_ref[...], (((0,), (0,)), ((), ())), preferred_element_type=jnp.float32
    )
    hidden = inputs_ref[...].astype(jnp.float32) + embedded
    normed = (layer_norm(hidden) * (1.0 + scale_ref[0]) + shift_ref[0]).astype(jnp.bfloat16)
    normed_ref[...] = normed
    low_ref[...] = jnp.dot(
        normed, factor_ref[...], preferred_element_type=jnp.float32
    ).astype(jnp.bfloat16)


def embed(kept, inputs, embed_weight, scale, shift, down_factor):
    keep_count, channels, total_rows = kept.shape
    width, rank = down_factor.shape
    block = 128
    blocks = total_rows // block
    whole = lambda *shape: pl.BlockSpec(shape, lambda k, b: (0,) * len(shape))
    one_row = pl.BlockSpec((1, 1, width), lambda k, b: (k, 0, 0))
    out_rows = lambda size: pl.BlockSpec((block, size), lambda k, b: (k * blocks + b, 0))
    return pl.pallas_call(
        embed_kernel,
        grid=(keep_count, blocks),
        in_specs=[
            pl.BlockSpec((1, channels, block), lambda k, b: (k, 0, b)),
            pl.BlockSpec((block, width), lambda k, b: (b, 0)),
            whole(channels, width),
            one_row,
            one_row,
            whole(width, rank),
        ],
        out_specs=[out_rows(width), out_rows(rank)],
        out_shape=[
            jax.ShapeDtypeStruct((keep_count * total_rows, width), jnp.bfloat16),
            jax.ShapeDtypeStruct((keep_count * total_rows, rank), jnp.bfloat16),
        ],
        compiler_params=pltpu.CompilerParams(vmem_limit_bytes=32 * 1024 * 1024),
        cost_estimate=pl.CostEstimate(
            flops=2 * keep_count * total_rows * width * (rank + channels),
            bytes_accessed=keep_count * total_rows * width * 4,
            transcendentals=0,
        ),
    )(kept, inputs, embed_weight, scale[:, None, :], shift[:, None, :], down_factor)


def attend_kernel(length_ref, q_ref, k_ref, v_ref, g_ref, low_ref, up_ref, dlow_ref, gup_ref):
    sample, head = pl.program_id(0), pl.program_id(1)
    total_rows = q_ref.shape[0]
    block_rows = min(512, total_rows)
    length = length_ref[0]
    factor = HEAD_DIM ** (-0.5)
    along = (((1,), (1,)), ((), ()))
    key_raw = k_ref[...]
    keys = norm_rows(key_raw).astype(jnp.bfloat16)
    values = v_ref[...].astype(jnp.bfloat16)
    up = up_ref[...]
    key_mask = lax.broadcasted_iota(jnp.int32, (1, total_rows), 1) < length
    for begin in range(0, total_rows, block_rows):
        rows = pl.ds(begin, block_rows)
        low = low_ref[rows, :]
        query = q_ref[rows, :] + jnp.dot(low, up, preferred_element_type=jnp.float32)
        inverse = lax.rsqrt(jnp.mean(query * query, -1, keepdims=True) + epsilon)
        normal = query * inverse
        row_mask = begin + lax.broadcasted_iota(jnp.int32, (block_rows, 1), 0) < length
        grad = jnp.where(row_mask, g_ref[0, rows, :].astype(jnp.float32), 0.0)
        grad_bf = grad.astype(jnp.bfloat16)
        scores = lax.dot_general(
            normal.astype(jnp.bfloat16), keys, along, preferred_element_type=jnp.float32
        )
        weights = jnp.where(key_mask, jnp.exp2(scores * (factor * math.log2(math.e))), 0.0)
        share = 1.0 / jnp.sum(weights, -1, keepdims=True)
        output = jnp.dot(
            weights.astype(jnp.bfloat16), values, preferred_element_type=jnp.float32
        )
        delta = jnp.sum(grad * output, -1, keepdims=True) * share
        grad_probs = lax.dot_general(
            grad_bf, values, along, preferred_element_type=jnp.float32
        )
        grad_scores = (weights * (grad_probs - delta)).astype(jnp.bfloat16)
        gradient = jnp.dot(grad_scores, keys, preferred_element_type=jnp.float32) * (share * factor)
        inner_mean = jnp.mean(gradient * normal, -1, keepdims=True)
        dquery = (inverse * (gradient - normal * inner_mean)).astype(jnp.bfloat16)
        part = lax.dot_general(dquery, up, along, preferred_element_type=jnp.float32)
        up_part = lax.dot_general(
            dquery, low, (((0,), (0,)), ((), ())), preferred_element_type=jnp.float32
        )

        @pl.when(head == 0)
        def _():
            dlow_ref[rows, :] = part

        @pl.when(head != 0)
        def _():
            dlow_ref[rows, :] += part

        place = pl.ds(pl.multiple_of(head * HEAD_DIM, HEAD_DIM), HEAD_DIM)

        @pl.when(jnp.logical_and(sample == 0, begin == 0))
        def _():
            gup_ref[place, :] = up_part

        @pl.when(jnp.logical_or(sample != 0, begin != 0))
        def _():
            gup_ref[place, :] += up_part


def attend(length, projected, grads, low, up):
    keep_count, total_rows, columns = grads.shape
    heads = columns // HEAD_DIM
    rank = up.shape[0]

    def column_block(first):
        return pl.BlockSpec((total_rows, HEAD_DIM), lambda k, h: (k, first + h))

    return pl.pallas_call(
        attend_kernel,
        grid=(keep_count, heads),
        in_specs=[
            pl.BlockSpec(memory_space=pltpu.SMEM),
            column_block(0),
            column_block(heads),
            column_block(2 * heads),
            pl.BlockSpec((1, total_rows, HEAD_DIM), lambda k, h: (k, 0, h)),
            pl.BlockSpec((total_rows, rank), lambda k, h: (k, 0)),
            pl.BlockSpec((rank, HEAD_DIM), lambda k, h: (0, h)),
        ],
        out_specs=[
            pl.BlockSpec((total_rows, rank), lambda k, h: (k, 0)),
            pl.BlockSpec((columns, rank), lambda k, h: (0, 0)),
        ],
        out_shape=[
            jax.ShapeDtypeStruct((keep_count * total_rows, rank), jnp.float32),
            jax.ShapeDtypeStruct((columns, rank), jnp.float32),
        ],
        compiler_params=pltpu.CompilerParams(vmem_limit_bytes=48 * 1024 * 1024),
    )(length, projected, projected, projected, grads, low, up)


def reduce_kernel(
    sizes, src_ref, down_ref, up_ref, in1, out2, in2, in3, send1, recv1, send2, recv2, send3, recv3
):
    pools, seqs, dps, rows, up_rows = sizes
    plane = pools * seqs
    per = seqs // dps
    wire = in1.dtype
    p, s, d = lax.axis_index("pool"), lax.axis_index("seq"), lax.axis_index("dp")
    me = p * seqs + s
    beside = [lax.rem(me + o, plane) for o in range(1, plane)]
    beside_id = [(j // seqs, lax.rem(j, seqs), d) for j in beside]
    across = [lax.rem(d + o, dps) for o in range(1, dps)]
    across_id = [(p, s, j) for j in across]
    barrier = pltpu.get_barrier_semaphore()
    for target in beside_id + across_id:
        pl.semaphore_signal(barrier, inc=1, device_id=target, device_id_type=pl.DeviceIdType.MESH)
    pl.semaphore_wait(barrier, plane - 1 + dps - 1)

    def copy(src, dst, send, recv, target):
        return pltpu.make_async_remote_copy(
            src_ref=src,
            dst_ref=dst,
            send_sem=send,
            recv_sem=recv,
            device_id=target,
            device_id_type=pl.DeviceIdType.MESH,
        )

    sends = []
    for j, target in zip(beside, beside_id):
        one = copy(src_ref.at[j], in1.at[me], send1.at[j], recv1.at[me], target)
        one.start()
        sends.append(one)
    in1[me] = src_ref[me]
    for j, target in zip(beside, beside_id):
        copy(src_ref.at[j], in1.at[j], send1.at[j], recv1.at[j], target).wait_recv()
    split = dps * rows
    total = in1[0, :split, :].astype(jnp.float32)
    for t in range(1, plane):
        total = total + in1[t, :split, :].astype(jnp.float32)
    for block in range(dps):
        ups = None
        for t in range(plane):
            if t % seqs // per == block:
                term = in1[t, split:, :].astype(jnp.float32)
                ups = term if ups is None else ups + term
        out2[block, :rows, :] = total[block * rows : (block + 1) * rows].astype(wire)
        out2[block, rows:, :] = ups.astype(wire)
    for j, target in zip(across, across_id):
        one = copy(out2.at[j], in2.at[d], send2.at[j], recv2.at[d], target)
        one.start()
        sends.append(one)
    in2[d] = out2[d]
    for j, target in zip(across, across_id):
        copy(out2.at[j], in2.at[j], send2.at[j], recv2.at[j], target).wait_recv()
    owned = in2[0].astype(jnp.float32)
    for t in range(1, dps):
        owned = owned + in2[t].astype(jnp.float32)
    in3[me] = owned.astype(wire)
    for j, target in zip(beside, beside_id):
        one = copy(in3.at[me], in3.at[me], send3.at[j], recv3.at[me], target)
        one.start()
        sends.append(one)
    for j, target in zip(beside, beside_id):
        copy(in3.at[j], in3.at[j], send3.at[j], recv3.at[j], target).wait_recv()
    for t in range(plane):
        down_ref[t * rows : (t + 1) * rows, :] = in3[t, :rows, :].astype(jnp.float32)
        up_ref[t * up_rows : (t + 1) * up_rows, :] = in3[t, rows:, :].astype(jnp.float32)
    for one in sends:
        one.wait_send()


def reduce_gradients(grad_down, grad_up_rows):
    pools, seqs, dps = (lax.axis_size(axis) for axis in ("pool", "seq", "dp"))
    plane = pools * seqs
    per = seqs // dps
    rank = grad_down.shape[1]
    down_rows = grad_down.shape[0] // dps
    own_up = grad_up_rows.shape[0]
    total_up = own_up * per
    rows, up_rows = down_rows // plane, total_up // plane
    wire = jnp.bfloat16 if rows % 16 == 0 and up_rows % 16 == 0 else jnp.float32
    if per > 1:
        here = lax.rem(lax.axis_index("seq"), per)
        grad_up_rows = lax.dynamic_update_slice_in_dim(
            jnp.zeros((total_up, rank), jnp.float32), grad_up_rows, here * own_up, 0
        )
    pieces = jnp.concatenate(
        [
            jnp.transpose(grad_down.reshape(dps, plane, rows, rank), (1, 0, 2, 3)).reshape(
                plane, dps * rows, rank
            ),
            grad_up_rows.reshape(plane, up_rows, rank),
        ],
        1,
    ).astype(wire)
    vmem = pl.BlockSpec(memory_space=pltpu.VMEM)
    dma = pltpu.SemaphoreType.DMA
    return pl.pallas_call(
        lambda *refs: reduce_kernel((pools, seqs, dps, rows, up_rows), *refs),
        in_specs=[vmem],
        out_specs=[vmem, vmem],
        out_shape=[
            jax.ShapeDtypeStruct((down_rows, rank), jnp.float32),
            jax.ShapeDtypeStruct((total_up, rank), jnp.float32),
        ],
        scratch_shapes=[
            pltpu.VMEM((plane, dps * rows + up_rows, rank), wire),
            pltpu.VMEM((dps, rows + up_rows, rank), wire),
            pltpu.VMEM((dps, rows + up_rows, rank), wire),
            pltpu.VMEM((plane, rows + up_rows, rank), wire),
            dma((plane,)),
            dma((plane,)),
            dma((dps,)),
            dma((dps,)),
            dma((plane,)),
            dma((plane,)),
        ],
        compiler_params=pltpu.CompilerParams(
            collective_id=1, has_side_effects=True, vmem_limit_bytes=48 * 1024 * 1024
        ),
    )(pieces)


def body_streamed(
    starting_latents,
    noise,
    velocity_matrix,
    kept_rollout_steps,
    trainer_group_of,
    video_valid_tokens,
    block_input_states,
    upstream,
    patch_embed_weight,
    modulation,
    frozen_query_key_value,
    query_down_factor,
    query_up_factor,
):
    halves = lax.axis_size("pool")
    groups = lax.axis_size("dp")
    half = lax.axis_index("pool")
    group = lax.axis_index("dp")
    videos = halves * groups
    video = half * groups + group
    video_ids = jnp.arange(videos, dtype=jnp.int32)
    steps_total = noise.shape[1]
    step_size = 1.0 / steps_total
    own_steps = jnp.sum(jnp.where((video_ids == video)[:, None], kept_rollout_steps, 0), 0)
    state = starting_latents[0].astype(jnp.float32)
    kept_rows = jnp.zeros((own_steps.shape[0],) + state.shape, jnp.float32)
    for step in range(steps_total):
        drift = jnp.dot(velocity_matrix, state, precision=lax.Precision.HIGHEST)
        state = (
            state
            - step_size * drift
            + noise_level * math.sqrt(step_size) * noise[0, step].astype(jnp.float32)
        )
        kept_rows = jnp.where((own_steps == step + 1)[:, None, None], state[None], kept_rows)
    kept_rows = kept_rows.astype(jnp.bfloat16)
    source_half = 1 - half
    trainer_row = jnp.sum(
        jnp.where(
            (jnp.arange(halves, dtype=jnp.int32) == source_half)[:, None], trainer_group_of, 0
        ),
        0,
    )
    source_group = jnp.sum(jnp.where(trainer_row == group, jnp.arange(groups, dtype=jnp.int32), 0))
    source = source_half * groups + source_group
    seqs = lax.axis_size("seq")
    place = lax.axis_index("seq")
    inner_width = query_up_factor.shape[1]
    columns = inner_width // seqs
    inputs_all = lax.all_gather(block_input_states[0], "seq", axis=0, tiled=True)
    grads_all = lax.all_to_all(upstream[0], "seq", split_axis=2, concat_axis=1, tiled=True)
    weight_rows = frozen_query_key_value.shape[0]
    own_weights = lax.dynamic_slice_in_dim(
        frozen_query_key_value.reshape(weight_rows, 3, inner_width), place * columns, columns, 2
    ).reshape(weight_rows, 3 * columns)
    weights = lax.all_gather(own_weights, ("pool", "dp"), axis=0, tiled=True)
    swapped = partner(kept_rows, "pool", 0)
    spread = lax.all_gather(swapped, ("dp", "seq"), axis=0)
    spread = spread.reshape((groups, seqs) + swapped.shape)
    received = lax.dynamic_index_in_dim(spread, source_group, 0, keepdims=False)
    received = jnp.transpose(received, (1, 2, 0, 3)).reshape(
        swapped.shape[0], swapped.shape[1], seqs * swapped.shape[2]
    )
    train_steps = jnp.sum(jnp.where((video_ids == source)[:, None], kept_rollout_steps, 0), 0)
    token_length = jnp.sum(jnp.where(video_ids == source, video_valid_tokens, 0))
    one_hot = (
        train_steps[:, None] - 1 == jnp.arange(steps_total, dtype=jnp.int32)[None, :]
    ).astype(jnp.float32)
    mod_scale = jnp.dot(one_hot, modulation[0], precision=lax.Precision.HIGHEST)
    mod_shift = jnp.dot(one_hot, modulation[1], precision=lax.Precision.HIGHEST)
    flattened_rows, low = embed(
        received, inputs_all, patch_embed_weight, mod_scale, mod_shift, query_down_factor
    )
    projected = jnp.dot(flattened_rows, weights, preferred_element_type=jnp.float32)
    own_up = lax.dynamic_slice_in_dim(query_up_factor, place * columns, columns, 1)
    gradient_low, grad_up_rows = attend(
        token_length.reshape(1), projected, grads_all, low, own_up
    )
    grad_down = lax.dot_general(
        flattened_rows,
        gradient_low.astype(jnp.bfloat16),
        (((0,), (0,)), ((), ())),
        preferred_element_type=jnp.float32,
    )
    owned_down, owned_up = reduce_gradients(grad_down, grad_up_rows)
    return (owned_down, owned_up.T, state[None])


def attend_slot(query, key_raw, values, grad, low, up, length):
    factor = HEAD_DIM ** (-0.5)
    along = (((1,), (1,)), ((), ()))
    total_rows = query.shape[0]
    keys = norm_rows(key_raw).astype(jnp.bfloat16)
    key_mask = lax.broadcasted_iota(jnp.int32, (1, total_rows), 1) < length
    row_mask = lax.broadcasted_iota(jnp.int32, (total_rows, 1), 0) < length
    inverse = lax.rsqrt(jnp.mean(query * query, -1, keepdims=True) + epsilon)
    normal = query * inverse
    grad = jnp.where(row_mask, grad.astype(jnp.float32), 0.0)
    scores = lax.dot_general(
        normal.astype(jnp.bfloat16), keys, along, preferred_element_type=jnp.float32
    )
    weights = jnp.where(key_mask, jnp.exp2(scores * (factor * math.log2(math.e))), 0.0)
    share = 1.0 / jnp.sum(weights, -1, keepdims=True)
    output = jnp.dot(weights.astype(jnp.bfloat16), values, preferred_element_type=jnp.float32)
    delta = jnp.sum(grad * output, -1, keepdims=True) * share
    grad_probs = lax.dot_general(
        grad.astype(jnp.bfloat16), values, along, preferred_element_type=jnp.float32
    )
    grad_scores = (weights * (grad_probs - delta)).astype(jnp.bfloat16)
    gradient = jnp.dot(grad_scores, keys, preferred_element_type=jnp.float32) * (share * factor)
    inner_mean = jnp.mean(gradient * normal, -1, keepdims=True)
    dquery = (inverse * (gradient - normal * inner_mean)).astype(jnp.bfloat16)
    dlow = lax.dot_general(dquery, up, along, preferred_element_type=jnp.float32)
    up_rows = lax.dot_general(
        dquery, low, (((0,), (0,)), ((), ())), preferred_element_type=jnp.float32
    )
    return dlow, up_rows


def step_kernel(
    sizes,
    steps_ref, trainer_ref, tokens_ref, start_ref, noise_ref, velocity_ref, inputs_ref,
    upstream_ref, embed_ref, modulation_ref, weight_ref, down_ref, up_ref,
    final_ref, normed_ref, dlow_ref, gup_ref,
    wall, xall, gall, kall, low_all, projected,
    local_w, local_x, local_g, send_w, recv_w, send_f, recv_f,
    send_x, recv_x, send_g, recv_g, send_k, recv_k,
):
    pools, seqs, dps = sizes
    keep_count, tok_rows = kall.shape[2], kall.shape[4]
    total_rows = seqs * tok_rows
    weight_rows = weight_ref.shape[0]
    inner_width = weight_ref.shape[1] // 3
    heads = wall.shape[0]
    columns = heads * HEAD_DIM
    p, s, d = lax.axis_index("pool"), lax.axis_index("seq"), lax.axis_index("dp")
    other = 1 - p
    mesh_type = pl.DeviceIdType.MESH
    seq_peers = [lax.rem(s + o, seqs) for o in range(1, seqs)]
    dp_peers = [lax.rem(d + o, dps) for o in range(1, dps)]
    greet = [(p, j, d) for j in seq_peers] + [(p, s, j) for j in dp_peers]
    greet += [(other, j, i) for i in range(dps) for j in range(seqs)]

    def block_rows(pool, group):
        return pl.ds(pl.multiple_of((pool * dps + group) * weight_rows, weight_rows), weight_rows)

    own_rows = block_rows(p, d)
    local = []
    for h in range(heads):
        for part in range(3):
            first = pl.multiple_of(part * inner_width + s * columns + h * HEAD_DIM, HEAD_DIM)
            local.append(
                pltpu.make_async_copy(
                    weight_ref.at[:, pl.ds(first, HEAD_DIM)],
                    wall.at[h, own_rows, pl.ds(part * HEAD_DIM, HEAD_DIM)],
                    local_w.at[h, part],
                )
            )
    local_inputs = pltpu.make_async_copy(inputs_ref.at[0], xall.at[s], local_x)

    def grads_of(j):
        return upstream_ref.at[0, :, :, pl.ds(pl.multiple_of(j * columns, columns), columns)]

    local_grads = pltpu.make_async_copy(grads_of(s), gall.at[s], local_g)
    for one in local + [local_inputs, local_grads]:
        one.start()
    barrier = pltpu.get_barrier_semaphore()
    for target in greet:
        pl.semaphore_signal(barrier, inc=1, device_id=target, device_id_type=mesh_type)
    pl.semaphore_wait(barrier, len(greet))

    def copy(src, dst, send, recv, target):
        return pltpu.make_async_remote_copy(
            src_ref=src,
            dst_ref=dst,
            send_sem=send,
            recv_sem=recv,
            device_id=target,
            device_id_type=mesh_type,
        )

    sends = []

    def launch(*args):
        one = copy(*args)
        one.start()
        sends.append(one)

    for one in local[:3]:
        one.wait()
    for j in dp_peers:
        launch(wall.at[0, own_rows], wall.at[0, own_rows], send_w.at[0, j], recv_w.at[0, d], (p, s, j))
    for j in seq_peers:
        launch(inputs_ref.at[0], xall.at[s], send_x.at[j], recv_x.at[s], (p, j, d))
    for one in local[3:]:
        one.wait()
    for h in range(1, heads):
        for j in dp_peers:
            launch(
                wall.at[h, own_rows], wall.at[h, own_rows], send_w.at[h, j], recv_w.at[h, d], (p, s, j)
            )
    for h in range(heads):
        launch(
            wall.at[h, own_rows], wall.at[h, own_rows], send_f.at[h, d], recv_f.at[h, d], (other, s, d)
        )
    for j in seq_peers:
        launch(grads_of(j), gall.at[s], send_g.at[j], recv_g.at[s], (p, j, d))

    video = p * dps + d
    steps_total = noise_ref.shape[1]
    step_size = 1.0 / steps_total
    state = start_ref[0].astype(jnp.float32)
    velocity = velocity_ref[...]
    kept_rows = [jnp.zeros_like(state) for _ in range(keep_count)]
    for step in range(steps_total):
        drift = jnp.dot(
            velocity, state, precision=lax.Precision.HIGHEST, preferred_element_type=jnp.float32
        )
        state = (
            state
            - step_size * drift
            + noise_level * math.sqrt(step_size) * noise_ref[0, step].astype(jnp.float32)
        )
        for k in range(keep_count):
            kept_rows[k] = jnp.where(steps_ref[video, k] == step + 1, state, kept_rows[k])
    final_ref[0] = state
    mine = seqs * dps
    for k in range(keep_count):
        kall[mine, 0, k] = kept_rows[k].astype(jnp.bfloat16)
    for i in range(dps):
        for j in range(seqs):
            launch(
                kall.at[mine, 0],
                kall.at[d * seqs + s, 0],
                send_k.at[i * seqs + j],
                recv_k.at[d * seqs + s],
                (other, j, i),
            )

    source_group = jnp.int32(0)
    for i in range(dps):
        source_group = jnp.where(trainer_ref[other, i] == d, i, source_group)
    source = other * dps + source_group
    length = tokens_ref[source]
    for i in range(dps):
        for j in range(seqs):
            spot = i * seqs + j
            copy(
                kall.at[mine, 0], kall.at[spot, 0], send_k.at[spot], recv_k.at[spot], (other, j, i)
            ).wait_recv()
    scales, shifts = [], []
    for k in range(keep_count):
        wanted = steps_ref[source, k]
        scale = jnp.zeros((1, normed_ref.shape[1]), jnp.float32)
        shift = scale
        for t in range(steps_total):
            scale = scale + jnp.where(wanted == t + 1, modulation_ref[0, t : t + 1, :], 0.0)
            shift = shift + jnp.where(wanted == t + 1, modulation_ref[1, t : t + 1, :], 0.0)
        scales.append(1.0 + scale)
        shifts.append(shift)
    local_inputs.wait()
    embed_weight = embed_ref[...]
    order = [s] + seq_peers
    for o, j in enumerate(order):
        if o > 0:
            copy(inputs_ref.at[0], xall.at[j], send_x.at[j], recv_x.at[j], (p, j, d)).wait_recv()
        for k in range(keep_count):
            kept = jnp.zeros(kall.shape[3:], jnp.float32)
            for i in range(dps):
                kept = kept + jnp.where(
                    source_group == i, kall[i * seqs + j, 0, k].astype(jnp.float32), 0.0
                )
            embedded = lax.dot_general(
                kept.astype(jnp.bfloat16),
                embed_weight,
                (((0,), (0,)), ((), ())),
                preferred_element_type=jnp.float32,
            )
            hidden = xall[j].astype(jnp.float32) + embedded
            normed = (layer_norm(hidden) * scales[k] + shifts[k]).astype(jnp.bfloat16)
            rows = pl.ds(pl.multiple_of(k * total_rows + j * tok_rows, tok_rows), tok_rows)
            normed_ref[rows, :] = normed
            low_all[rows, :] = jnp.dot(
                normed, down_ref[...], preferred_element_type=jnp.float32
            ).astype(jnp.bfloat16)

    local_grads.wait()
    for j in seq_peers:
        copy(grads_of(j), gall.at[j], send_g.at[j], recv_g.at[j], (p, j, d)).wait_recv()
    for h in range(heads):
        for j in dp_peers:
            there = block_rows(p, j)
            copy(
                wall.at[h, there], wall.at[h, there], send_w.at[h, j], recv_w.at[h, j], (p, s, j)
            ).wait_recv()
            launch(
                wall.at[h, there], wall.at[h, there], send_f.at[h, j], recv_f.at[h, j], (other, s, d)
            )
        for j in [d] + dp_peers:
            there = block_rows(other, j)
            copy(
                wall.at[h, there], wall.at[h, there], send_f.at[h, j], recv_f.at[h, j], (other, s, d)
            ).wait_recv()
        up = up_ref[:, pl.ds(pl.multiple_of(s * columns + h * HEAD_DIM, HEAD_DIM), HEAD_DIM)]
        gup = None
        for k in range(keep_count):
            rows = slice(k * total_rows, (k + 1) * total_rows)
            projected[...] = jnp.dot(
                normed_ref[rows, :], wall[h], preferred_element_type=jnp.float32
            )
            low = low_all[rows, :]
            query = projected[:, :HEAD_DIM] + jnp.dot(low, up, preferred_element_type=jnp.float32)
            grad = gall[:, k, :, h * HEAD_DIM : (h + 1) * HEAD_DIM].reshape(total_rows, HEAD_DIM)
            dlow, up_rows = attend_slot(
                query,
                projected[:, HEAD_DIM : 2 * HEAD_DIM],
                projected[:, 2 * HEAD_DIM :].astype(jnp.bfloat16),
                grad,
                low,
                up,
                length,
            )
            dlow_ref[rows, :] = dlow if h == 0 else dlow_ref[rows, :] + dlow
            gup = up_rows if gup is None else gup + up_rows
        gup_ref[h * HEAD_DIM : (h + 1) * HEAD_DIM, :] = gup
    for one in sends:
        one.wait_send()


def train_step(*arguments):
    (
        steps, trainer, tokens, start, noise, velocity, inputs, upstream, embed_weight,
        modulation, weight, down, up,
    ) = arguments
    pools, seqs, dps = (lax.axis_size(axis) for axis in ("pool", "seq", "dp"))
    keep_count, tok_rows = upstream.shape[1:3]
    channels = start.shape[1]
    width, rank = down.shape
    inner_width = up.shape[1]
    columns = inner_width // seqs
    heads = columns // HEAD_DIM
    total_rows = seqs * tok_rows
    vmem = pl.BlockSpec(memory_space=pltpu.VMEM)
    smem = pl.BlockSpec(memory_space=pltpu.SMEM)
    hbm = pl.BlockSpec(memory_space=pl.ANY)
    dma = pltpu.SemaphoreType.DMA
    bf = jnp.bfloat16
    return pl.pallas_call(
        lambda *refs: step_kernel((pools, seqs, dps), *refs),
        in_specs=[smem] * 3 + [vmem] * 3 + [hbm] * 2 + [vmem] * 2 + [hbm] + [vmem] * 2,
        out_specs=[vmem] * 4,
        out_shape=[
            jax.ShapeDtypeStruct((1, channels, tok_rows), jnp.float32),
            jax.ShapeDtypeStruct((keep_count * total_rows, width), bf),
            jax.ShapeDtypeStruct((keep_count * total_rows, rank), jnp.float32),
            jax.ShapeDtypeStruct((columns, rank), jnp.float32),
        ],
        scratch_shapes=[
            pltpu.VMEM((heads, width, 3 * HEAD_DIM), bf),
            pltpu.VMEM((seqs, tok_rows, width), bf),
            pltpu.VMEM((seqs, keep_count, tok_rows, columns), bf),
            pltpu.VMEM((seqs * dps + 1, 1, keep_count, channels, tok_rows), bf),
            pltpu.VMEM((keep_count * total_rows, rank), bf),
            pltpu.VMEM((total_rows, 3 * HEAD_DIM), jnp.float32),
            dma((heads, 3)),
            dma,
            dma,
            dma((heads, dps)),
            dma((heads, dps)),
            dma((heads, dps)),
            dma((heads, dps)),
            dma((seqs,)),
            dma((seqs,)),
            dma((seqs,)),
            dma((seqs,)),
            dma((seqs * dps,)),
            dma((seqs * dps,)),
        ],
        compiler_params=pltpu.CompilerParams(
            collective_id=2, has_side_effects=True, vmem_limit_bytes=56 * 1024 * 1024
        ),
    )(*arguments)


def body_in_vmem(
    starting_latents,
    noise,
    velocity_matrix,
    kept_rollout_steps,
    trainer_group_of,
    video_valid_tokens,
    block_input_states,
    upstream,
    patch_embed_weight,
    modulation,
    frozen_query_key_value,
    query_down_factor,
    query_up_factor,
):
    final, normed, gradient_low, grad_up_rows = train_step(
        kept_rollout_steps,
        trainer_group_of,
        video_valid_tokens,
        starting_latents,
        noise,
        velocity_matrix,
        block_input_states,
        upstream,
        patch_embed_weight,
        modulation,
        frozen_query_key_value,
        query_down_factor,
        query_up_factor,
    )
    grad_down = lax.dot_general(
        normed,
        gradient_low.astype(jnp.bfloat16),
        (((0,), (0,)), ((), ())),
        preferred_element_type=jnp.float32,
    )
    owned_down, owned_up = reduce_gradients(grad_down, grad_up_rows)
    return (owned_down, owned_up.T, final)


def solution(mesh):
    def body(*arguments):
        tokens = arguments[6].shape[1] * lax.axis_size("seq")
        return (body_in_vmem if tokens <= 512 else body_streamed)(*arguments)

    return jax.shard_map(
        body,
        mesh=mesh,
        in_specs=(
            P(("pool", "dp"), None, "seq"),
            P(("pool", "dp"), None, None, "seq"),
            P(),
            P(),
            P(),
            P(),
            P(("pool", "dp"), "seq", None),
            P(("pool", "dp"), None, "seq", None),
            P(),
            P(),
            P(("pool", "dp"), None),
            P(),
            P(),
        ),
        out_specs=(P("dp", None), P(None, "dp"), P(("pool", "dp"), None, "seq")),
        check_vma=False,
    )
```

```python
import math

import jax
import jax.numpy as jnp
from jax import lax
from jax.experimental import pallas as pl
from jax.experimental.pallas import tpu as pltpu
from jax.sharding import PartitionSpec as P

HEADS = 16
HEAD_DIM = 128


epsilon = 1e-06
noise_level = 0.5


def partner(block, axis, apart):
    count = lax.axis_size(axis)
    route = []
    for low in range(count):
        high = low | 1 << apart
        if high != low and high < count:
            route += [(low, high), (high, low)]
    return lax.ppermute(block, axis, route)


def norm_rows(values):
    return values * lax.rsqrt(jnp.mean(values * values, -1, keepdims=True) + epsilon)


def layer_norm(values):
    centered = values - jnp.mean(values, -1, keepdims=True)
    return centered * lax.rsqrt(jnp.mean(centered * centered, -1, keepdims=True) + epsilon)


def embed_kernel(kept_ref, inputs_ref, embed_ref, scale_ref, shift_ref, factor_ref, normed_ref, low_ref):
    embedded = lax.dot_general(
        kept_ref[0], embed_ref[...], (((0,), (0,)), ((), ())), preferred_element_type=jnp.float32
    )
    hidden = inputs_ref[...].astype(jnp.float32) + embedded
    normed = (layer_norm(hidden) * (1.0 + scale_ref[0]) + shift_ref[0]).astype(jnp.bfloat16)
    normed_ref[...] = normed
    low_ref[...] = jnp.dot(
        normed, factor_ref[...], preferred_element_type=jnp.float32
    ).astype(jnp.bfloat16)


def embed(kept, inputs, embed_weight, scale, shift, down_factor):
    keep_count, channels, total_rows = kept.shape
    width, rank = down_factor.shape
    block = 128
    blocks = total_rows // block
    whole = lambda *shape: pl.BlockSpec(shape, lambda k, b: (0,) * len(shape))
    one_row = pl.BlockSpec((1, 1, width), lambda k, b: (k, 0, 0))
    out_rows = lambda size: pl.BlockSpec((block, size), lambda k, b: (k * blocks + b, 0))
    return pl.pallas_call(
        embed_kernel,
        grid=(keep_count, blocks),
        in_specs=[
            pl.BlockSpec((1, channels, block), lambda k, b: (k, 0, b)),
            pl.BlockSpec((block, width), lambda k, b: (b, 0)),
            whole(channels, width),
            one_row,
            one_row,
            whole(width, rank),
        ],
        out_specs=[out_rows(width), out_rows(rank)],
        out_shape=[
            jax.ShapeDtypeStruct((keep_count * total_rows, width), jnp.bfloat16),
            jax.ShapeDtypeStruct((keep_count * total_rows, rank), jnp.bfloat16),
        ],
        compiler_params=pltpu.CompilerParams(vmem_limit_bytes=32 * 1024 * 1024),
        cost_estimate=pl.CostEstimate(
            flops=2 * keep_count * total_rows * width * (rank + channels),
            bytes_accessed=keep_count * total_rows * width * 4,
            transcendentals=0,
        ),
    )(kept, inputs, embed_weight, scale[:, None, :], shift[:, None, :], down_factor)


def attend_kernel(length_ref, q_ref, k_ref, v_ref, g_ref, low_ref, up_ref, dlow_ref, gup_ref):
    sample, head = pl.program_id(0), pl.program_id(1)
    total_rows = q_ref.shape[0]
    block_rows = min(512, total_rows)
    length = length_ref[0]
    factor = HEAD_DIM ** (-0.5)
    along = (((1,), (1,)), ((), ()))
    key_raw = k_ref[...]
    keys = norm_rows(key_raw).astype(jnp.bfloat16)
    values = v_ref[...].astype(jnp.bfloat16)
    up = up_ref[...]
    key_mask = lax.broadcasted_iota(jnp.int32, (1, total_rows), 1) < length
    for begin in range(0, total_rows, block_rows):
        rows = pl.ds(begin, block_rows)
        low = low_ref[rows, :]
        query = q_ref[rows, :] + jnp.dot(low, up, preferred_element_type=jnp.float32)
        inverse = lax.rsqrt(jnp.mean(query * query, -1, keepdims=True) + epsilon)
        normal = query * inverse
        row_mask = begin + lax.broadcasted_iota(jnp.int32, (block_rows, 1), 0) < length
        grad = jnp.where(row_mask, g_ref[0, rows, :].astype(jnp.float32), 0.0)
        grad_bf = grad.astype(jnp.bfloat16)
        scores = lax.dot_general(
            normal.astype(jnp.bfloat16), keys, along, preferred_element_type=jnp.float32
        )
        weights = jnp.where(key_mask, jnp.exp2(scores * (factor * math.log2(math.e))), 0.0)
        share = 1.0 / jnp.sum(weights, -1, keepdims=True)
        output = jnp.dot(
            weights.astype(jnp.bfloat16), values, preferred_element_type=jnp.float32
        )
        delta = jnp.sum(grad * output, -1, keepdims=True) * share
        grad_probs = lax.dot_general(
            grad_bf, values, along, preferred_element_type=jnp.float32
        )
        grad_scores = (weights * (grad_probs - delta)).astype(jnp.bfloat16)
        gradient = jnp.dot(grad_scores, keys, preferred_element_type=jnp.float32) * (share * factor)
        inner_mean = jnp.mean(gradient * normal, -1, keepdims=True)
        dquery = (inverse * (gradient - normal * inner_mean)).astype(jnp.bfloat16)
        part = lax.dot_general(dquery, up, along, preferred_element_type=jnp.float32)
        up_part = lax.dot_general(
            dquery, low, (((0,), (0,)), ((), ())), preferred_element_type=jnp.float32
        )

        @pl.when(head == 0)
        def _():
            dlow_ref[rows, :] = part

        @pl.when(head != 0)
        def _():
            dlow_ref[rows, :] += part

        place = pl.ds(pl.multiple_of(head * HEAD_DIM, HEAD_DIM), HEAD_DIM)

        @pl.when(jnp.logical_and(sample == 0, begin == 0))
        def _():
            gup_ref[place, :] = up_part

        @pl.when(jnp.logical_or(sample != 0, begin != 0))
        def _():
            gup_ref[place, :] += up_part


def attend(length, projected, grads, low, up):
    keep_count, total_rows, columns = grads.shape
    heads = columns // HEAD_DIM
    rank = up.shape[0]

    def column_block(first):
        return pl.BlockSpec((total_rows, HEAD_DIM), lambda k, h: (k, first + h))

    return pl.pallas_call(
        attend_kernel,
        grid=(keep_count, heads),
        in_specs=[
            pl.BlockSpec(memory_space=pltpu.SMEM),
            column_block(0),
            column_block(heads),
            column_block(2 * heads),
            pl.BlockSpec((1, total_rows, HEAD_DIM), lambda k, h: (k, 0, h)),
            pl.BlockSpec((total_rows, rank), lambda k, h: (k, 0)),
            pl.BlockSpec((rank, HEAD_DIM), lambda k, h: (0, h)),
        ],
        out_specs=[
            pl.BlockSpec((total_rows, rank), lambda k, h: (k, 0)),
            pl.BlockSpec((columns, rank), lambda k, h: (0, 0)),
        ],
        out_shape=[
            jax.ShapeDtypeStruct((keep_count * total_rows, rank), jnp.float32),
            jax.ShapeDtypeStruct((columns, rank), jnp.float32),
        ],
        compiler_params=pltpu.CompilerParams(vmem_limit_bytes=48 * 1024 * 1024),
    )(length, projected, projected, projected, grads, low, up)


def reduce_kernel(
    sizes, src_ref, down_ref, up_ref, in1, out2, in2, in3, send1, recv1, send2, recv2, send3, recv3
):
    pools, seqs, dps, rows, up_rows = sizes
    plane = pools * seqs
    per = seqs // dps
    wire = in1.dtype
    p, s, d = lax.axis_index("pool"), lax.axis_index("seq"), lax.axis_index("dp")
    me = p * seqs + s
    beside = [lax.rem(me + o, plane) for o in range(1, plane)]
    beside_id = [(j // seqs, lax.rem(j, seqs), d) for j in beside]
    across = [lax.rem(d + o, dps) for o in range(1, dps)]
    across_id = [(p, s, j) for j in across]
    barrier = pltpu.get_barrier_semaphore()
    for target in beside_id + across_id:
        pl.semaphore_signal(barrier, inc=1, device_id=target, device_id_type=pl.DeviceIdType.MESH)
    pl.semaphore_wait(barrier, plane - 1 + dps - 1)

    def copy(src, dst, send, recv, target):
        return pltpu.make_async_remote_copy(
            src_ref=src,
            dst_ref=dst,
            send_sem=send,
            recv_sem=recv,
            device_id=target,
            device_id_type=pl.DeviceIdType.MESH,
        )

    sends = []
    for j, target in zip(beside, beside_id):
        one = copy(src_ref.at[j], in1.at[me], send1.at[j], recv1.at[me], target)
        one.start()
        sends.append(one)
    in1[me] = src_ref[me]
    for j, target in zip(beside, beside_id):
        copy(src_ref.at[j], in1.at[j], send1.at[j], recv1.at[j], target).wait_recv()
    split = dps * rows
    total = in1[0, :split, :].astype(jnp.float32)
    for t in range(1, plane):
        total = total + in1[t, :split, :].astype(jnp.float32)
    for block in range(dps):
        ups = None
        for t in range(plane):
            if t % seqs // per == block:
                term = in1[t, split:, :].astype(jnp.float32)
                ups = term if ups is None else ups + term
        out2[block, :rows, :] = total[block * rows : (block + 1) * rows].astype(wire)
        out2[block, rows:, :] = ups.astype(wire)
    for j, target in zip(across, across_id):
        one = copy(out2.at[j], in2.at[d], send2.at[j], recv2.at[d], target)
        one.start()
        sends.append(one)
    in2[d] = out2[d]
    for j, target in zip(across, across_id):
        copy(out2.at[j], in2.at[j], send2.at[j], recv2.at[j], target).wait_recv()
    owned = in2[0].astype(jnp.float32)
    for t in range(1, dps):
        owned = owned + in2[t].astype(jnp.float32)
    in3[me] = owned.astype(wire)
    for j, target in zip(beside, beside_id):
        one = copy(in3.at[me], in3.at[me], send3.at[j], recv3.at[me], target)
        one.start()
        sends.append(one)
    for j, target in zip(beside, beside_id):
        copy(in3.at[j], in3.at[j], send3.at[j], recv3.at[j], target).wait_recv()
    for t in range(plane):
        down_ref[t * rows : (t + 1) * rows, :] = in3[t, :rows, :].astype(jnp.float32)
        up_ref[t * up_rows : (t + 1) * up_rows, :] = in3[t, rows:, :].astype(jnp.float32)
    for one in sends:
        one.wait_send()


def reduce_gradients(grad_down, grad_up_rows):
    pools, seqs, dps = (lax.axis_size(axis) for axis in ("pool", "seq", "dp"))
    plane = pools * seqs
    per = seqs // dps
    rank = grad_down.shape[1]
    down_rows = grad_down.shape[0] // dps
    own_up = grad_up_rows.shape[0]
    total_up = own_up * per
    rows, up_rows = down_rows // plane, total_up // plane
    wire = jnp.bfloat16 if rows % 16 == 0 and up_rows % 16 == 0 else jnp.float32
    if per > 1:
        here = lax.rem(lax.axis_index("seq"), per)
        grad_up_rows = lax.dynamic_update_slice_in_dim(
            jnp.zeros((total_up, rank), jnp.float32), grad_up_rows, here * own_up, 0
        )
    pieces = jnp.concatenate(
        [
            jnp.transpose(grad_down.reshape(dps, plane, rows, rank), (1, 0, 2, 3)).reshape(
                plane, dps * rows, rank
            ),
            grad_up_rows.reshape(plane, up_rows, rank),
        ],
        1,
    ).astype(wire)
    vmem = pl.BlockSpec(memory_space=pltpu.VMEM)
    dma = pltpu.SemaphoreType.DMA
    return pl.pallas_call(
        lambda *refs: reduce_kernel((pools, seqs, dps, rows, up_rows), *refs),
        in_specs=[vmem],
        out_specs=[vmem, vmem],
        out_shape=[
            jax.ShapeDtypeStruct((down_rows, rank), jnp.float32),
            jax.ShapeDtypeStruct((total_up, rank), jnp.float32),
        ],
        scratch_shapes=[
            pltpu.VMEM((plane, dps * rows + up_rows, rank), wire),
            pltpu.VMEM((dps, rows + up_rows, rank), wire),
            pltpu.VMEM((dps, rows + up_rows, rank), wire),
            pltpu.VMEM((plane, rows + up_rows, rank), wire),
            dma((plane,)),
            dma((plane,)),
            dma((dps,)),
            dma((dps,)),
            dma((plane,)),
            dma((plane,)),
        ],
        compiler_params=pltpu.CompilerParams(
            collective_id=1, has_side_effects=True, vmem_limit_bytes=48 * 1024 * 1024
        ),
    )(pieces)


def body_streamed(
    starting_latents,
    noise,
    velocity_matrix,
    kept_rollout_steps,
    trainer_group_of,
    video_valid_tokens,
    block_input_states,
    upstream,
    patch_embed_weight,
    modulation,
    frozen_query_key_value,
    query_down_factor,
    query_up_factor,
):
    halves = lax.axis_size("pool")
    groups = lax.axis_size("dp")
    half = lax.axis_index("pool")
    group = lax.axis_index("dp")
    videos = halves * groups
    video = half * groups + group
    video_ids = jnp.arange(videos, dtype=jnp.int32)
    steps_total = noise.shape[1]
    step_size = 1.0 / steps_total
    own_steps = jnp.sum(jnp.where((video_ids == video)[:, None], kept_rollout_steps, 0), 0)
    state = starting_latents[0].astype(jnp.float32)
    kept_rows = jnp.zeros((own_steps.shape[0],) + state.shape, jnp.float32)
    for step in range(steps_total):
        drift = jnp.dot(velocity_matrix, state, precision=lax.Precision.HIGHEST)
        state = (
            state
            - step_size * drift
            + noise_level * math.sqrt(step_size) * noise[0, step].astype(jnp.float32)
        )
        kept_rows = jnp.where((own_steps == step + 1)[:, None, None], state[None], kept_rows)
    kept_rows = kept_rows.astype(jnp.bfloat16)
    source_half = 1 - half
    trainer_row = jnp.sum(
        jnp.where(
            (jnp.arange(halves, dtype=jnp.int32) == source_half)[:, None], trainer_group_of, 0
        ),
        0,
    )
    source_group = jnp.sum(jnp.where(trainer_row == group, jnp.arange(groups, dtype=jnp.int32), 0))
    source = source_half * groups + source_group
    seqs = lax.axis_size("seq")
    place = lax.axis_index("seq")
    inner_width = query_up_factor.shape[1]
    columns = inner_width // seqs
    inputs_all = lax.all_gather(block_input_states[0], "seq", axis=0, tiled=True)
    grads_all = lax.all_to_all(upstream[0], "seq", split_axis=2, concat_axis=1, tiled=True)
    weight_rows = frozen_query_key_value.shape[0]
    own_weights = lax.dynamic_slice_in_dim(
        frozen_query_key_value.reshape(weight_rows, 3, inner_width), place * columns, columns, 2
    ).reshape(weight_rows, 3 * columns)
    weights = lax.all_gather(own_weights, ("pool", "dp"), axis=0, tiled=True)
    swapped = partner(kept_rows, "pool", 0)
    spread = lax.all_gather(swapped, ("dp", "seq"), axis=0)
    spread = spread.reshape((groups, seqs) + swapped.shape)
    received = lax.dynamic_index_in_dim(spread, source_group, 0, keepdims=False)
    received = jnp.transpose(received, (1, 2, 0, 3)).reshape(
        swapped.shape[0], swapped.shape[1], seqs * swapped.shape[2]
    )
    train_steps = jnp.sum(jnp.where((video_ids == source)[:, None], kept_rollout_steps, 0), 0)
    token_length = jnp.sum(jnp.where(video_ids == source, video_valid_tokens, 0))
    one_hot = (
        train_steps[:, None] - 1 == jnp.arange(steps_total, dtype=jnp.int32)[None, :]
    ).astype(jnp.float32)
    mod_scale = jnp.dot(one_hot, modulation[0], precision=lax.Precision.HIGHEST)
    mod_shift = jnp.dot(one_hot, modulation[1], precision=lax.Precision.HIGHEST)
    flattened_rows, low = embed(
        received, inputs_all, patch_embed_weight, mod_scale, mod_shift, query_down_factor
    )
    projected = jnp.dot(flattened_rows, weights, preferred_element_type=jnp.float32)
    own_up = lax.dynamic_slice_in_dim(query_up_factor, place * columns, columns, 1)
    gradient_low, grad_up_rows = attend(
        token_length.reshape(1), projected, grads_all, low, own_up
    )
    grad_down = lax.dot_general(
        flattened_rows,
        gradient_low.astype(jnp.bfloat16),
        (((0,), (0,)), ((), ())),
        preferred_element_type=jnp.float32,
    )
    owned_down, owned_up = reduce_gradients(grad_down, grad_up_rows)
    return (owned_down, owned_up.T, state[None])


def attend_slot(query, key_raw, values, grad, low, up, length):
    factor = HEAD_DIM ** (-0.5)
    along = (((1,), (1,)), ((), ()))
    total_rows = query.shape[0]
    keys = norm_rows(key_raw).astype(jnp.bfloat16)
    key_mask = lax.broadcasted_iota(jnp.int32, (1, total_rows), 1) < length
    row_mask = lax.broadcasted_iota(jnp.int32, (total_rows, 1), 0) < length
    inverse = lax.rsqrt(jnp.mean(query * query, -1, keepdims=True) + epsilon)
    normal = query * inverse
    grad = jnp.where(row_mask, grad.astype(jnp.float32), 0.0)
    scores = lax.dot_general(
        normal.astype(jnp.bfloat16), keys, along, preferred_element_type=jnp.float32
    )
    weights = jnp.where(key_mask, jnp.exp2(scores * (factor * math.log2(math.e))), 0.0)
    share = 1.0 / jnp.sum(weights, -1, keepdims=True)
    output = jnp.dot(weights.astype(jnp.bfloat16), values, preferred_element_type=jnp.float32)
    delta = jnp.sum(grad * output, -1, keepdims=True) * share
    grad_probs = lax.dot_general(
        grad.astype(jnp.bfloat16), values, along, preferred_element_type=jnp.float32
    )
    grad_scores = (weights * (grad_probs - delta)).astype(jnp.bfloat16)
    gradient = jnp.dot(grad_scores, keys, preferred_element_type=jnp.float32) * (share * factor)
    inner_mean = jnp.mean(gradient * normal, -1, keepdims=True)
    dquery = (inverse * (gradient - normal * inner_mean)).astype(jnp.bfloat16)
    dlow = lax.dot_general(dquery, up, along, preferred_element_type=jnp.float32)
    up_rows = lax.dot_general(
        dquery, low, (((0,), (0,)), ((), ())), preferred_element_type=jnp.float32
    )
    return dlow, up_rows


def step_kernel(
    sizes,
    steps_ref, trainer_ref, tokens_ref, start_ref, noise_ref, velocity_ref, inputs_ref,
    upstream_ref, embed_ref, modulation_ref, weight_ref, down_ref, up_ref,
    final_ref, normed_ref, dlow_ref, gup_ref,
    wall, xall, gall, kall, low_all, projected,
    local_w, local_x, local_g, send_w, recv_w, send_f, recv_f,
    send_x, recv_x, send_g, recv_g, send_k, recv_k,
):
    pools, seqs, dps = sizes
    keep_count, tok_rows = kall.shape[2], kall.shape[4]
    total_rows = seqs * tok_rows
    weight_rows = weight_ref.shape[0]
    inner_width = weight_ref.shape[1] // 3
    heads = wall.shape[0]
    columns = heads * HEAD_DIM
    p, s, d = lax.axis_index("pool"), lax.axis_index("seq"), lax.axis_index("dp")
    other = 1 - p
    mesh_type = pl.DeviceIdType.MESH
    seq_peers = [lax.rem(s + o, seqs) for o in range(1, seqs)]
    dp_peers = [lax.rem(d + o, dps) for o in range(1, dps)]
    greet = [(p, j, d) for j in seq_peers] + [(p, s, j) for j in dp_peers]
    greet += [(other, j, i) for i in range(dps) for j in range(seqs)]

    def block_rows(pool, group):
        return pl.ds(pl.multiple_of((pool * dps + group) * weight_rows, weight_rows), weight_rows)

    own_rows = block_rows(p, d)
    local = []
    for h in range(heads):
        for part in range(3):
            first = pl.multiple_of(part * inner_width + s * columns + h * HEAD_DIM, HEAD_DIM)
            local.append(
                pltpu.make_async_copy(
                    weight_ref.at[:, pl.ds(first, HEAD_DIM)],
                    wall.at[h, own_rows, pl.ds(part * HEAD_DIM, HEAD_DIM)],
                    local_w.at[h, part],
                )
            )
    local_inputs = pltpu.make_async_copy(inputs_ref.at[0], xall.at[s], local_x)

    def grads_of(j):
        return upstream_ref.at[0, :, :, pl.ds(pl.multiple_of(j * columns, columns), columns)]

    local_grads = pltpu.make_async_copy(grads_of(s), gall.at[s], local_g)
    for one in local + [local_inputs, local_grads]:
        one.start()
    barrier = pltpu.get_barrier_semaphore()
    for target in greet:
        pl.semaphore_signal(barrier, inc=1, device_id=target, device_id_type=mesh_type)
    pl.semaphore_wait(barrier, len(greet))

    def copy(src, dst, send, recv, target):
        return pltpu.make_async_remote_copy(
            src_ref=src,
            dst_ref=dst,
            send_sem=send,
            recv_sem=recv,
            device_id=target,
            device_id_type=mesh_type,
        )

    sends = []

    def launch(*args):
        one = copy(*args)
        one.start()
        sends.append(one)

    video = p * dps + d
    steps_total = noise_ref.shape[1]
    step_size = 1.0 / steps_total
    state = start_ref[0].astype(jnp.float32)
    velocity = velocity_ref[...]
    kept_rows = [jnp.zeros_like(state) for _ in range(keep_count)]
    for step in range(steps_total):
        drift = jnp.dot(
            velocity, state, precision=lax.Precision.HIGHEST, preferred_element_type=jnp.float32
        )
        state = (
            state
            - step_size * drift
            + noise_level * math.sqrt(step_size) * noise_ref[0, step].astype(jnp.float32)
        )
        for k in range(keep_count):
            kept_rows[k] = jnp.where(steps_ref[video, k] == step + 1, state, kept_rows[k])
    final_ref[0] = state
    mine = seqs * dps
    for k in range(keep_count):
        kall[mine, 0, k] = kept_rows[k].astype(jnp.bfloat16)
    for i in range(dps):
        for j in range(seqs):
            launch(
                kall.at[mine, 0],
                kall.at[d * seqs + s, 0],
                send_k.at[i * seqs + j],
                recv_k.at[d * seqs + s],
                (other, j, i),
            )

    for one in local[:3]:
        one.wait()
    for j in dp_peers:
        launch(wall.at[0, own_rows], wall.at[0, own_rows], send_w.at[0, j], recv_w.at[0, d], (p, s, j))
    for j in seq_peers:
        launch(inputs_ref.at[0], xall.at[s], send_x.at[j], recv_x.at[s], (p, j, d))
    for one in local[3:]:
        one.wait()
    for h in range(1, heads):
        for j in dp_peers:
            launch(
                wall.at[h, own_rows], wall.at[h, own_rows], send_w.at[h, j], recv_w.at[h, d], (p, s, j)
            )
    for h in range(heads):
        launch(
            wall.at[h, own_rows], wall.at[h, own_rows], send_f.at[h, d], recv_f.at[h, d], (other, s, d)
        )
    for j in seq_peers:
        launch(grads_of(j), gall.at[s], send_g.at[j], recv_g.at[s], (p, j, d))

    source_group = jnp.int32(0)
    for i in range(dps):
        source_group = jnp.where(trainer_ref[other, i] == d, i, source_group)
    source = other * dps + source_group
    length = tokens_ref[source]
    for i in range(dps):
        for j in range(seqs):
            spot = i * seqs + j
            copy(
                kall.at[mine, 0], kall.at[spot, 0], send_k.at[spot], recv_k.at[spot], (other, j, i)
            ).wait_recv()
    scales, shifts = [], []
    for k in range(keep_count):
        wanted = steps_ref[source, k]
        scale = jnp.zeros((1, normed_ref.shape[1]), jnp.float32)
        shift = scale
        for t in range(steps_total):
            scale = scale + jnp.where(wanted == t + 1, modulation_ref[0, t : t + 1, :], 0.0)
            shift = shift + jnp.where(wanted == t + 1, modulation_ref[1, t : t + 1, :], 0.0)
        scales.append(1.0 + scale)
        shifts.append(shift)
    local_inputs.wait()
    embed_weight = embed_ref[...]
    order = [s] + seq_peers
    for o, j in enumerate(order):
        if o > 0:
            copy(inputs_ref.at[0], xall.at[j], send_x.at[j], recv_x.at[j], (p, j, d)).wait_recv()
        for k in range(keep_count):
            kept = jnp.zeros(kall.shape[3:], jnp.float32)
            for i in range(dps):
                kept = kept + jnp.where(
                    source_group == i, kall[i * seqs + j, 0, k].astype(jnp.float32), 0.0
                )
            embedded = lax.dot_general(
                kept.astype(jnp.bfloat16),
                embed_weight,
                (((0,), (0,)), ((), ())),
                preferred_element_type=jnp.float32,
            )
            hidden = xall[j].astype(jnp.float32) + embedded
            normed = (layer_norm(hidden) * scales[k] + shifts[k]).astype(jnp.bfloat16)
            rows = pl.ds(pl.multiple_of(k * total_rows + j * tok_rows, tok_rows), tok_rows)
            normed_ref[rows, :] = normed
            low_all[rows, :] = jnp.dot(
                normed, down_ref[...], preferred_element_type=jnp.float32
            ).astype(jnp.bfloat16)

    local_grads.wait()
    for j in seq_peers:
        copy(grads_of(j), gall.at[j], send_g.at[j], recv_g.at[j], (p, j, d)).wait_recv()
    for h in range(heads):
        for j in dp_peers:
            there = block_rows(p, j)
            copy(
                wall.at[h, there], wall.at[h, there], send_w.at[h, j], recv_w.at[h, j], (p, s, j)
            ).wait_recv()
            launch(
                wall.at[h, there], wall.at[h, there], send_f.at[h, j], recv_f.at[h, j], (other, s, d)
            )
        for j in [d] + dp_peers:
            there = block_rows(other, j)
            copy(
                wall.at[h, there], wall.at[h, there], send_f.at[h, j], recv_f.at[h, j], (other, s, d)
            ).wait_recv()
        up = up_ref[:, pl.ds(pl.multiple_of(s * columns + h * HEAD_DIM, HEAD_DIM), HEAD_DIM)]
        gup = None
        for k in range(keep_count):
            rows = slice(k * total_rows, (k + 1) * total_rows)
            projected[...] = jnp.dot(
                normed_ref[rows, :], wall[h], preferred_element_type=jnp.float32
            )
            low = low_all[rows, :]
            query = projected[:, :HEAD_DIM] + jnp.dot(low, up, preferred_element_type=jnp.float32)
            grad = gall[:, k, :, h * HEAD_DIM : (h + 1) * HEAD_DIM].reshape(total_rows, HEAD_DIM)
            dlow, up_rows = attend_slot(
                query,
                projected[:, HEAD_DIM : 2 * HEAD_DIM],
                projected[:, 2 * HEAD_DIM :].astype(jnp.bfloat16),
                grad,
                low,
                up,
                length,
            )
            dlow_ref[rows, :] = dlow if h == 0 else dlow_ref[rows, :] + dlow
            gup = up_rows if gup is None else gup + up_rows
        gup_ref[h * HEAD_DIM : (h + 1) * HEAD_DIM, :] = gup
    for one in sends:
        one.wait_send()


def train_step(*arguments):
    (
        steps, trainer, tokens, start, noise, velocity, inputs, upstream, embed_weight,
        modulation, weight, down, up,
    ) = arguments
    pools, seqs, dps = (lax.axis_size(axis) for axis in ("pool", "seq", "dp"))
    keep_count, tok_rows = upstream.shape[1:3]
    channels = start.shape[1]
    width, rank = down.shape
    inner_width = up.shape[1]
    columns = inner_width // seqs
    heads = columns // HEAD_DIM
    total_rows = seqs * tok_rows
    vmem = pl.BlockSpec(memory_space=pltpu.VMEM)
    smem = pl.BlockSpec(memory_space=pltpu.SMEM)
    hbm = pl.BlockSpec(memory_space=pl.ANY)
    dma = pltpu.SemaphoreType.DMA
    bf = jnp.bfloat16
    return pl.pallas_call(
        lambda *refs: step_kernel((pools, seqs, dps), *refs),
        in_specs=[smem] * 3 + [vmem] * 3 + [hbm] * 2 + [vmem] * 2 + [hbm] + [vmem] * 2,
        out_specs=[vmem] * 4,
        out_shape=[
            jax.ShapeDtypeStruct((1, channels, tok_rows), jnp.float32),
            jax.ShapeDtypeStruct((keep_count * total_rows, width), bf),
            jax.ShapeDtypeStruct((keep_count * total_rows, rank), jnp.float32),
            jax.ShapeDtypeStruct((columns, rank), jnp.float32),
        ],
        scratch_shapes=[
            pltpu.VMEM((heads, width, 3 * HEAD_DIM), bf),
            pltpu.VMEM((seqs, tok_rows, width), bf),
            pltpu.VMEM((seqs, keep_count, tok_rows, columns), bf),
            pltpu.VMEM((seqs * dps + 1, 1, keep_count, channels, tok_rows), bf),
            pltpu.VMEM((keep_count * total_rows, rank), bf),
            pltpu.VMEM((total_rows, 3 * HEAD_DIM), jnp.float32),
            dma((heads, 3)),
            dma,
            dma,
            dma((heads, dps)),
            dma((heads, dps)),
            dma((heads, dps)),
            dma((heads, dps)),
            dma((seqs,)),
            dma((seqs,)),
            dma((seqs,)),
            dma((seqs,)),
            dma((seqs * dps,)),
            dma((seqs * dps,)),
        ],
        compiler_params=pltpu.CompilerParams(
            collective_id=2, has_side_effects=True, vmem_limit_bytes=56 * 1024 * 1024
        ),
    )(*arguments)


def body_in_vmem(
    starting_latents,
    noise,
    velocity_matrix,
    kept_rollout_steps,
    trainer_group_of,
    video_valid_tokens,
    block_input_states,
    upstream,
    patch_embed_weight,
    modulation,
    frozen_query_key_value,
    query_down_factor,
    query_up_factor,
):
    final, normed, gradient_low, grad_up_rows = train_step(
        kept_rollout_steps,
        trainer_group_of,
        video_valid_tokens,
        starting_latents,
        noise,
        velocity_matrix,
        block_input_states,
        upstream,
        patch_embed_weight,
        modulation,
        frozen_query_key_value,
        query_down_factor,
        query_up_factor,
    )
    grad_down = lax.dot_general(
        normed,
        gradient_low.astype(jnp.bfloat16),
        (((0,), (0,)), ((), ())),
        preferred_element_type=jnp.float32,
    )
    owned_down, owned_up = reduce_gradients(grad_down, grad_up_rows)
    return (owned_down, owned_up.T, final)


def solution(mesh):
    def body(*arguments):
        tokens = arguments[6].shape[1] * lax.axis_size("seq")
        return (body_in_vmem if tokens <= 512 else body_streamed)(*arguments)

    return jax.shard_map(
        body,
        mesh=mesh,
        in_specs=(
            P(("pool", "dp"), None, "seq"),
            P(("pool", "dp"), None, None, "seq"),
            P(),
            P(),
            P(),
            P(),
            P(("pool", "dp"), "seq", None),
            P(("pool", "dp"), None, "seq", None),
            P(),
            P(),
            P(("pool", "dp"), None),
            P(),
            P(),
        ),
        out_specs=(P("dp", None), P(None, "dp"), P(("pool", "dp"), None, "seq")),
        check_vma=False,
    )
```
